256 devices in a mesh: gx: 16 (over y, z_hi, core), gy: 16 (over x, z_lo).
Axes of the slice: x: 4, y: 4, z: 8 (z_hi: 2, z_lo: 4; z = z_hi * 4 + z_lo), core: 2. Of those that a mesh axis runs over, the one named last changes fastest.
Arguments:
- queries: bfloat16 [2, 4, 40, 128], replicated, may hold values from -120 to 120
- keys: bfloat16 [2, 131072, 8, 128], P(None, ('gx', 'gy')), may hold values from -6 to 6
- values: bfloat16 [2, 131072, 8, 128], P(None, ('gx', 'gy')), may hold values from -6 to 6
Outputs:
- attended: bfloat16 [2, 4, 40, 128], replicated
The draws below stay inside these ranges and needn't reach their ends.
All inputs are finite; a program needn't handle non-finite values.
Results may differ from the reference program's by a relative error of at most 0.0011.
Values sent between devices are 32-bit elements; how exact they have to be, the bound alone decides.
No kernel may reach another device: no remote copies, remote signals or barrier semaphores. Data moves between devices by JAX's collectives and lax.ppermute only.
A program may use at most 128 MiB of HBM per device.

```python
import jax
import jax.numpy as jnp
from jax import lax

QH = 40
KVH = 8
HD = 128
SEQS = 2
QTOK = 4
KV_DEV = 512
LENGTH = 131072


def weak_dims(key):
    picks = jax.random.randint(jax.random.fold_in(key, 103), (SEQS, KVH, HD), 0, 4)
    return (picks == 0).astype(jnp.float32)


def draw_queries(key, part):
    base_key = key
    key = jax.random.fold_in(key, 1)
    weak = jnp.repeat(weak_dims(base_key), QH // KVH, axis=1)[:, None, :, :]
    spread = 3.5 + 20.5 * weak
    drawn = jnp.clip(jax.random.normal(key, (SEQS, QTOK, QH, HD), jnp.float32) * spread, -96.0, 96.0)
    return drawn.astype(jnp.bfloat16)


def draw_keys(key, part):
    base_key = key
    key = jax.random.fold_in(key, 2)
    key_scale = (1.0 - 0.97 * weak_dims(base_key))[:, None, :, :]
    drawn = jnp.clip(jax.random.normal(key, (SEQS, LENGTH, KVH, HD), jnp.float32), -6.0, 6.0) * key_scale
    return drawn.astype(jnp.bfloat16)


def block_scale(stream_key, extent, shards, smallest, high):
    def one(dim, blocks):
        draws = jax.random.uniform(jax.random.fold_in(jax.random.fold_in(stream_key, 6), dim), (blocks,), jnp.float32, smallest / len(shards), high / len(shards))
        return jnp.repeat(jnp.exp(draws), extent[dim] // blocks).reshape((-1,) + (1,) * (len(extent) - dim - 1))

    factor_of = one(*shards[0])
    for cut in shards[1:]:
        factor_of = factor_of * one(*cut)
    return factor_of


def noise(rng, dims, scale, reach, pieces=(), kind=jnp.bfloat16):
    entries = jax.random.normal(rng, dims, jnp.float32) * scale
    if len(pieces) > 0:
        entries = block_scale(rng, dims, pieces, -0.22, 0.18) * entries
    return jnp.clip(entries, min=-reach, max=reach).astype(kind)


def setup_inputs(seed: int = 0) -> dict:
    splits = jax.random.split(jax.random.key(seed), 4)
    return {
        "queries": draw_queries(jax.random.fold_in(splits[3], 71), 0),
        "keys": draw_keys(jax.random.fold_in(splits[3], 71), 0),
        "values": noise(splits[2], (SEQS, LENGTH, KVH, HD), 1.0, 6.0, ((1, 256),)),
    }


def reference(queries, keys, values):
    scaling = HD ** -0.5
    group_size = QH // KVH
    grouped = queries.reshape(SEQS, QTOK, KVH, group_size, HD).astype(jnp.float32)
    block_count = LENGTH // KV_DEV

    def one_block(block_index):
        offset = (block_index * KV_DEV).astype(jnp.int32)
        key_block = lax.dynamic_slice_in_dim(keys, offset, KV_DEV, 1).astype(jnp.float32)
        value_block = lax.dynamic_slice_in_dim(values, offset, KV_DEV, 1).astype(jnp.float32)
        scores = jnp.einsum("sqgrd,stgd->sqgrt", grouped, key_block) * scaling
        block_max = jnp.max(scores, axis=-1)
        weights = jnp.exp(scores - block_max[..., None])
        block_total = jnp.sum(weights, axis=-1)
        rounded_weights = weights.astype(jnp.bfloat16).astype(jnp.float32)
        block_out = jnp.einsum("sqgrt,stgd->sqgrd", rounded_weights, value_block)
        return block_out, block_max, block_total

    outputs, maxima, totals = lax.map(one_block, jnp.arange(block_count, dtype=jnp.int32))
    peak = jnp.max(maxima, axis=0)
    factors = jnp.exp(maxima - peak[None])
    numerator = jnp.sum(outputs * factors[..., None], axis=0)
    denominator = jnp.sum(totals * factors, axis=0)
    attended = numerator / denominator[..., None]
    return attended.reshape(SEQS, QTOK, QH, HD).astype(jnp.bfloat16)
```

```python
import functools
import math

import jax
import jax.numpy as jnp
from jax import lax
from jax.experimental import pallas as pl
from jax.experimental.pallas import tpu as pltpu
from jax.sharding import PartitionSpec as P

QH = 40
KVH = 8
HD = 128
SEQS = 2
QTOK = 4
ROWS = QTOK * QH
PIECES = 16
PIECE = SEQS * ROWS // PIECES
BLOCK = 24
MAX_ROW = PIECE
TOTAL_ROW = PIECE + 1
SCALE_LOG2 = HD ** (-0.5) * math.log2(math.e)
CHUNK = 512
AXES = ("gx", "gy")
MIB = 1 << 20


def device_index(core, x, y, z):
    return ((y * 2 + z // 4) * 2 + core) * 16 + x * 4 + z % 4


SPREAD = [
    [device_index(core, x, 2 * half + (side ^ half), z) for core in range(2) for x in range(4) for side in range(2)]
    for half in range(2)
    for z in range(8)
]
HOLDERS = [
    [device_index(core, x, y, z) for y in pair for z in range(8)]
    for core in range(2)
    for x in range(4)
    for pair in ((0, 3), (1, 2))
]


def attend_kernel(q_ref, k_hbm, v_hbm, out_ref, k_buf, v_buf, scores, rows, stats, sems):
    count = k_buf.shape[1]
    copies = []
    for s in range(SEQS):
        copies.append(
            (
                pltpu.make_async_copy(k_hbm.at[s], k_buf.at[s], sems.at[2 * s]),
                pltpu.make_async_copy(v_hbm.at[s], v_buf.at[s], sems.at[2 * s + 1]),
            )
        )
    for pair in copies:
        for copy in pair:
            copy.start()
    row = lax.broadcasted_iota(jnp.int32, (ROWS, CHUNK), 0)
    lane = lax.broadcasted_iota(jnp.int32, (ROWS, CHUNK), 1)
    own_head = (row % QH) // (QH // KVH) == lane % KVH
    diagonal = row[:, :HD] % PIECE == lane[:, :HD]
    out_ref[:, PIECE:BLOCK, :] = jnp.zeros((PIECES, BLOCK - PIECE, HD), jnp.float32)
    for s in range(SEQS):
        copies[s][0].wait()
        highest = jnp.full((ROWS, HD), -1e30, jnp.float32)
        for j in range(0, count, CHUNK):
            part = lax.dot_general(
                q_ref[s],
                k_buf[s, pl.ds(j, CHUNK), :],
                (((1,), (1,)), ((), ())),
                preferred_element_type=jnp.float32,
            )
            part = jnp.where(own_head, part, -1e30)
            scores[:, pl.ds(j, CHUNK)] = part
            for i in range(0, CHUNK, HD):
                highest = jnp.maximum(highest, part[:, i : i + HD])
        block_max = jnp.max(highest, axis=1, keepdims=True)
        copies[s][1].wait()
        total = jnp.zeros((ROWS, HD), jnp.float32)
        block_out = jnp.zeros((ROWS, HD), jnp.float32)
        for j in range(0, count, CHUNK):
            weights = jnp.exp2((scores[:, pl.ds(j, CHUNK)] - block_max) * SCALE_LOG2)
            for i in range(0, CHUNK, HD):
                total = total + weights[:, i : i + HD]
            block_out = block_out + jnp.dot(
                weights.astype(jnp.bfloat16),
                v_buf[s, pl.ds(j, CHUNK), :],
                preferred_element_type=jnp.float32,
            )
        block_total = jnp.sum(total, axis=1, keepdims=True)
        rows[...] = block_out
        stats[0] = jnp.where(diagonal, block_max, 0.0)
        stats[1] = jnp.where(diagonal, block_total, 0.0)
        for p in range(ROWS // PIECE):
            at = s * (ROWS // PIECE) + p
            own = pl.ds(p * PIECE, PIECE)
            out_ref[at, 0:PIECE, :] = rows[own, :]
            out_ref[at, MAX_ROW : MAX_ROW + 1, :] = jnp.sum(stats[0, own, :], axis=0, keepdims=True)
            out_ref[at, TOTAL_ROW : TOTAL_ROW + 1, :] = jnp.sum(stats[1, own, :], axis=0, keepdims=True)


def attend(queries, keys, values):
    count = keys.shape[1]
    return pl.pallas_call(
        attend_kernel,
        out_shape=jax.ShapeDtypeStruct((PIECES, BLOCK, HD), jnp.float32),
        in_specs=[
            pl.BlockSpec(memory_space=pltpu.VMEM),
            pl.BlockSpec(memory_space=pltpu.HBM),
            pl.BlockSpec(memory_space=pltpu.HBM),
        ],
        out_specs=pl.BlockSpec(memory_space=pltpu.VMEM),
        scratch_shapes=[
            pltpu.VMEM((SEQS, count, HD), jnp.bfloat16),
            pltpu.VMEM((SEQS, count, HD), jnp.bfloat16),
            pltpu.VMEM((ROWS, count), jnp.float32),
            pltpu.VMEM((ROWS, HD), jnp.float32),
            pltpu.VMEM((2, ROWS, HD), jnp.float32),
            pltpu.SemaphoreType.DMA((2 * SEQS,)),
        ],
        compiler_params=pltpu.CompilerParams(vmem_limit_bytes=32 * MIB),
        name="attend",
    )(queries, keys, values)


def merge_kernel(last, parts_ref, out_ref):
    n = parts_ref.shape[0]
    maxima = parts_ref[:, MAX_ROW, :]
    highest = jnp.max(maxima, axis=0, keepdims=True)
    factors = jnp.exp2((maxima - highest) * SCALE_LOG2)
    total = jnp.sum(factors * parts_ref[:, TOTAL_ROW, :], axis=0, keepdims=True)
    by_row = jnp.transpose(jnp.concatenate([factors, jnp.broadcast_to(total, (8, HD))], axis=0))
    by_row = by_row[:BLOCK]
    merged = jnp.zeros((BLOCK, HD), jnp.float32)
    for i in range(n):
        merged = merged + parts_ref[i] * by_row[:, i : i + 1]
    row = lax.broadcasted_iota(jnp.int32, (BLOCK, HD), 0)
    if last:
        merged = jnp.where(row < PIECE, merged / by_row[:, n : n + 1], 0.0)
    else:
        merged = jnp.where(row < PIECE, merged, jnp.where(row == MAX_ROW, highest, total))
    for i in range(out_ref.shape[0]):
        out_ref[i] = merged


def merge(parts, copies, last):
    return pl.pallas_call(
        functools.partial(merge_kernel, last),
        out_shape=jax.ShapeDtypeStruct((copies, BLOCK, HD), jnp.float32),
        in_specs=[pl.BlockSpec(memory_space=pltpu.VMEM)],
        out_specs=pl.BlockSpec(memory_space=pltpu.VMEM),
        name="merge_last" if last else "merge",
    )(parts)


def finish_kernel(pieces_ref, out_ref):
    for s in range(SEQS):
        for q in range(QTOK):
            at = (s * QTOK + q) * (QH // PIECE)
            whole = [pieces_ref[at + i, 0:PIECE, :] for i in range(QH // PIECE)]
            out_ref[s, q] = jnp.concatenate(whole, axis=0).astype(jnp.bfloat16)


def finish(pieces):
    return pl.pallas_call(
        finish_kernel,
        out_shape=jax.ShapeDtypeStruct((SEQS, QTOK, QH, HD), jnp.bfloat16),
        in_specs=[pl.BlockSpec(memory_space=pltpu.VMEM)],
        out_specs=pl.BlockSpec(memory_space=pltpu.VMEM),
        name="finish",
    )(pieces)


def exchange(blocks, groups):
    return lax.all_to_all(blocks, AXES, 0, 0, tiled=True, axis_index_groups=groups)


def per_device(queries, keys, values):
    count = keys.shape[1] * KVH
    partials = attend(
        queries.reshape(SEQS, ROWS, HD),
        keys.reshape(SEQS, count, HD),
        values.reshape(SEQS, count, HD),
    )
    mine = merge(exchange(partials, SPREAD), len(HOLDERS[0]), False)
    done = merge(exchange(mine, HOLDERS), len(SPREAD[0]), True)
    return finish(exchange(done, SPREAD))


def solution(mesh):
    placed = (P(), P(None, AXES, None, None), P(None, AXES, None, None))
    return jax.shard_map(per_device, mesh=mesh, in_specs=placed, out_specs=P(), check_vma=False)
```

```python
import functools
import math

import jax
import jax.numpy as jnp
from jax import lax
from jax.experimental import pallas as pl
from jax.experimental.pallas import tpu as pltpu
from jax.sharding import PartitionSpec as P

QH = 40
KVH = 8
HD = 128
SEQS = 2
QTOK = 4
ROWS = QTOK * QH
PIECES = 16
PIECE = SEQS * ROWS // PIECES
BLOCK = 24
MAX_ROW = PIECE
TOTAL_ROW = PIECE + 1
SCALE_LOG2 = HD ** (-0.5) * math.log2(math.e)
CHUNK = 512
LOWEST = -1e30
AXES = ("gx", "gy")
MIB = 1 << 20


def device_index(core, x, y, z):
    return ((y * 2 + z // 4) * 2 + core) * 16 + x * 4 + z % 4


SPREAD = [
    [device_index(core, 2 * half + (side ^ half), y, z) for core in range(2) for y in range(4) for side in range(2)]
    for half in range(2)
    for z in range(8)
]
HOLDERS = [
    [device_index(core, x, y, z) for x in pair for z in range(7, -1, -1)]
    for core in range(2)
    for y in range(4)
    for pair in ((0, 3), (1, 2))
]


def attend_kernel(q_hbm, k_hbm, v_hbm, out_ref, q_buf, k_buf, v_buf, scores, rows, stats, q_sem, k_sem, v_sem):
    count = k_buf.shape[1]
    q_copy = pltpu.make_async_copy(q_hbm, q_buf, q_sem)
    k_copy = [pltpu.make_async_copy(k_hbm.at[s], k_buf.at[s], k_sem.at[s]) for s in range(SEQS)]
    v_copy = [pltpu.make_async_copy(v_hbm.at[s], v_buf.at[s], v_sem.at[s]) for s in range(SEQS)]
    q_copy.start()
    for s in range(SEQS):
        k_copy[s].start()
        v_copy[s].start()
    row = lax.broadcasted_iota(jnp.int32, (ROWS, HD), 0)
    lane = lax.broadcasted_iota(jnp.int32, (ROWS, HD), 1)
    own_head = (row % QH) // (QH // KVH) == lane % KVH
    bias = jnp.where(own_head, 0.0, LOWEST).astype(jnp.float32)
    diagonal = row % PIECE == lane
    zero = jnp.zeros((ROWS, HD), jnp.float32)
    out_ref[:, PIECE:BLOCK, :] = jnp.zeros((PIECES, BLOCK - PIECE, HD), jnp.float32)

    def score(s, j, highest):
        part = lax.dot_general(
            q_buf[s],
            k_buf[s, pl.ds(j, CHUNK), :],
            (((1,), (1,)), ((), ())),
            preferred_element_type=jnp.float32,
        )
        for i in range(0, CHUNK, HD):
            own = part[:, i : i + HD] + bias
            scores[s, :, pl.ds(j + i, HD)] = own
            highest = jnp.maximum(highest, own)
        return highest

    def weigh(s, j, block_max, total, block_out):
        weights = jnp.exp2((scores[s, :, pl.ds(j, CHUNK)] - block_max) * SCALE_LOG2)
        for i in range(0, CHUNK, HD):
            total = total + weights[:, i : i + HD]
        block_out = block_out + jnp.dot(
            weights.astype(jnp.bfloat16),
            v_buf[s, pl.ds(j, CHUNK), :],
            preferred_element_type=jnp.float32,
        )
        return total, block_out

    def write(s, block_max, total, block_out):
        rows[s] = block_out
        stats[s, 0] = jnp.where(diagonal, block_max, 0.0)
        stats[s, 1] = jnp.where(diagonal, jnp.sum(total, axis=1, keepdims=True), 0.0)
        for p in range(ROWS // PIECE):
            at = s * (ROWS // PIECE) + p
            own = pl.ds(p * PIECE, PIECE)
            out_ref[at, 0:PIECE, :] = rows[s, own, :]
            out_ref[at, MAX_ROW : MAX_ROW + 1, :] = jnp.sum(stats[s, 0, own, :], axis=0, keepdims=True)
            out_ref[at, TOTAL_ROW : TOTAL_ROW + 1, :] = jnp.sum(stats[s, 1, own, :], axis=0, keepdims=True)

    q_copy.wait()
    k_copy[0].wait()
    highest = jnp.full((ROWS, HD), LOWEST, jnp.float32)
    for j in range(0, count, CHUNK):
        highest = score(0, j, highest)
    block_max = jnp.max(highest, axis=1, keepdims=True)
    for s in range(SEQS):
        if s + 1 < SEQS:
            k_copy[s + 1].wait()
        v_copy[s].wait()
        highest = jnp.full((ROWS, HD), LOWEST, jnp.float32)
        total, block_out = zero, zero
        for j in range(0, count, CHUNK):
            if s + 1 < SEQS:
                highest = score(s + 1, j, highest)
            total, block_out = weigh(s, j, block_max, total, block_out)
        write(s, block_max, total, block_out)
        block_max = jnp.max(highest, axis=1, keepdims=True)


def attend(queries, keys, values):
    count = keys.shape[1]
    return pl.pallas_call(
        attend_kernel,
        out_shape=jax.ShapeDtypeStruct((PIECES, BLOCK, HD), jnp.float32),
        in_specs=[pl.BlockSpec(memory_space=pltpu.HBM)] * 3,
        out_specs=pl.BlockSpec(memory_space=pltpu.VMEM),
        scratch_shapes=[
            pltpu.VMEM((SEQS, ROWS, HD), jnp.bfloat16),
            pltpu.VMEM((SEQS, count, HD), jnp.bfloat16),
            pltpu.VMEM((SEQS, count, HD), jnp.bfloat16),
            pltpu.VMEM((SEQS, ROWS, count), jnp.float32),
            pltpu.VMEM((SEQS, ROWS, HD), jnp.float32),
            pltpu.VMEM((SEQS, 2, ROWS, HD), jnp.float32),
            pltpu.SemaphoreType.DMA,
            pltpu.SemaphoreType.DMA((SEQS,)),
            pltpu.SemaphoreType.DMA((SEQS,)),
        ],
        compiler_params=pltpu.CompilerParams(vmem_limit_bytes=60 * MIB),
        name="attend",
    )(queries, keys, values)


def merge_kernel(last, parts_ref, out_ref):
    n = parts_ref.shape[0]
    maxima = parts_ref[:, MAX_ROW, :]
    highest = jnp.max(maxima, axis=0, keepdims=True)
    factors = jnp.exp2((maxima - highest) * SCALE_LOG2)
    total = jnp.sum(factors * parts_ref[:, TOTAL_ROW, :], axis=0, keepdims=True)
    by_row = jnp.transpose(jnp.concatenate([factors, jnp.broadcast_to(total, (8, HD))], axis=0))
    by_row = by_row[:BLOCK]
    merged = jnp.zeros((BLOCK, HD), jnp.float32)
    for i in range(n):
        merged = merged + parts_ref[i] * by_row[:, i : i + 1]
    row = lax.broadcasted_iota(jnp.int32, (BLOCK, HD), 0)
    if last:
        merged = jnp.where(row < PIECE, merged / by_row[:, n : n + 1], 0.0)
    else:
        merged = jnp.where(row < PIECE, merged, jnp.where(row == MAX_ROW, highest, total))
    for i in range(out_ref.shape[0]):
        out_ref[i] = merged


def merge(parts, copies, last):
    return pl.pallas_call(
        functools.partial(merge_kernel, last),
        out_shape=jax.ShapeDtypeStruct((copies, BLOCK, HD), jnp.float32),
        in_specs=[pl.BlockSpec(memory_space=pltpu.VMEM)],
        out_specs=pl.BlockSpec(memory_space=pltpu.VMEM),
        compiler_params=pltpu.CompilerParams(vmem_limit_bytes=4 * MIB),
        name="merge_last" if last else "merge",
    )(parts)


def finish_kernel(pieces_ref, out_ref):
    for s in range(SEQS):
        for q in range(QTOK):
            at = (s * QTOK + q) * (QH // PIECE)
            whole = [pieces_ref[at + i, 0:PIECE, :] for i in range(QH // PIECE)]
            out_ref[s, q] = jnp.concatenate(whole, axis=0).astype(jnp.bfloat16)


def finish(pieces):
    return pl.pallas_call(
        finish_kernel,
        out_shape=jax.ShapeDtypeStruct((SEQS, QTOK, QH, HD), jnp.bfloat16),
        in_specs=[pl.BlockSpec(memory_space=pltpu.VMEM)],
        out_specs=pl.BlockSpec(memory_space=pltpu.VMEM),
        compiler_params=pltpu.CompilerParams(vmem_limit_bytes=4 * MIB),
        name="finish",
    )(pieces)


def exchange(blocks, groups):
    return lax.all_to_all(blocks, AXES, 0, 0, tiled=True, axis_index_groups=groups)


def per_device(queries, keys, values):
    count = keys.shape[1] * KVH
    partials = attend(
        queries.reshape(SEQS, ROWS, HD),
        keys.reshape(SEQS, count, HD),
        values.reshape(SEQS, count, HD),
    )
    mine = merge(exchange(partials, SPREAD), len(HOLDERS[0]), False)
    done = merge(exchange(mine, HOLDERS), len(SPREAD[0]), True)
    return finish(exchange(done, SPREAD))


def solution(mesh):
    placed = (P(), P(None, AXES, None, None), P(None, AXES, None, None))
    return jax.shard_map(per_device, mesh=mesh, in_specs=placed, out_specs=P(), check_vma=False)
```

```python
import functools
import math

import jax
import jax.numpy as jnp
from jax import lax
from jax.experimental import pallas as pl
from jax.experimental.pallas import tpu as pltpu
from jax.sharding import PartitionSpec as P

QH = 40
KVH = 8
HD = 128
SEQS = 2
QTOK = 4
ROWS = QTOK * QH
PIECES = 16
PIECE = SEQS * ROWS // PIECES
BLOCK = 24
MAX_ROW = PIECE
TOTAL_ROW = PIECE + 1
SCALE_LOG2 = HD ** (-0.5) * math.log2(math.e)
CHUNK = 512
LOWEST = -1e30
AXES = ("gx", "gy")
MIB = 1 << 20


def device_index(core, x, y, z):
    return ((y * 2 + z // 4) * 2 + core) * 16 + x * 4 + z % 4


SPREAD = [
    [device_index(core, x, y, z) for x in (2, 1, 3, 0) for y in pair for core in (1, 0)]
    for pair in ((1, 0), (2, 3))
    for z in range(8)
]
HOLDERS = [
    [device_index(core, x, y, z) for z in (4, 3, 5, 2, 6, 1, 7, 0) for y in pair]
    for core in range(2)
    for x in range(4)
    for pair in ((2, 1), (3, 0))
]


def attend_kernel(q_hbm, k_hbm, v_hbm, out_ref, q_buf, k_buf, v_buf, scores, rows, stats, q_sem, k_sem, v_sem):
    count = k_buf.shape[1]
    q_copy = pltpu.make_async_copy(q_hbm, q_buf, q_sem)
    k_copy = [pltpu.make_async_copy(k_hbm.at[s], k_buf.at[s], k_sem.at[s]) for s in range(SEQS)]
    v_copy = [pltpu.make_async_copy(v_hbm.at[s], v_buf.at[s], v_sem.at[s]) for s in range(SEQS)]
    q_copy.start()
    for s in range(SEQS):
        k_copy[s].start()
        v_copy[s].start()
    row = lax.broadcasted_iota(jnp.int32, (ROWS, HD), 0)
    lane = lax.broadcasted_iota(jnp.int32, (ROWS, HD), 1)
    own_head = (row % QH) // (QH // KVH) == lane % KVH
    bias = jnp.where(own_head, 0.0, LOWEST).astype(jnp.float32)
    diagonal = row % PIECE == lane
    zero = jnp.zeros((ROWS, HD), jnp.float32)
    out_ref[:, PIECE:BLOCK, :] = jnp.zeros((PIECES, BLOCK - PIECE, HD), jnp.float32)

    def score(s, j, highest):
        part = lax.dot_general(
            q_buf[s],
            k_buf[s, pl.ds(j, CHUNK), :],
            (((1,), (1,)), ((), ())),
            preferred_element_type=jnp.float32,
        )
        for i in range(0, CHUNK, HD):
            own = part[:, i : i + HD] + bias
            scores[s, :, pl.ds(j + i, HD)] = own
            highest = jnp.maximum(highest, own)
        return highest

    def weigh(s, j, block_max, total, block_out):
        weights = jnp.exp2((scores[s, :, pl.ds(j, CHUNK)] - block_max) * SCALE_LOG2)
        for i in range(0, CHUNK, HD):
            total = total + weights[:, i : i + HD]
        block_out = block_out + jnp.dot(
            weights.astype(jnp.bfloat16),
            v_buf[s, pl.ds(j, CHUNK), :],
            preferred_element_type=jnp.float32,
        )
        return total, block_out

    def write(s, block_max, total, block_out):
        rows[s] = block_out
        stats[s, 0] = jnp.where(diagonal, block_max, 0.0)
        stats[s, 1] = jnp.where(diagonal, jnp.sum(total, axis=1, keepdims=True), 0.0)
        for p in range(ROWS // PIECE):
            at = s * (ROWS // PIECE) + p
            own = pl.ds(p * PIECE, PIECE)
            out_ref[at, 0:PIECE, :] = rows[s, own, :]
            out_ref[at, MAX_ROW : MAX_ROW + 1, :] = jnp.sum(stats[s, 0, own, :], axis=0, keepdims=True)
            out_ref[at, TOTAL_ROW : TOTAL_ROW + 1, :] = jnp.sum(stats[s, 1, own, :], axis=0, keepdims=True)

    q_copy.wait()
    k_copy[0].wait()
    highest = jnp.full((ROWS, HD), LOWEST, jnp.float32)
    for j in range(0, count, CHUNK):
        highest = score(0, j, highest)
    block_max = jnp.max(highest, axis=1, keepdims=True)
    for s in range(SEQS):
        if s + 1 < SEQS:
            k_copy[s + 1].wait()
        v_copy[s].wait()
        highest = jnp.full((ROWS, HD), LOWEST, jnp.float32)
        total, block_out = zero, zero
        for j in range(0, count, CHUNK):
            if s + 1 < SEQS:
                highest = score(s + 1, j, highest)
            total, block_out = weigh(s, j, block_max, total, block_out)
        write(s, block_max, total, block_out)
        block_max = jnp.max(highest, axis=1, keepdims=True)


def attend(queries, keys, values):
    count = keys.shape[1]
    return pl.pallas_call(
        attend_kernel,
        out_shape=jax.ShapeDtypeStruct((PIECES, BLOCK, HD), jnp.float32),
        in_specs=[pl.BlockSpec(memory_space=pltpu.HBM)] * 3,
        out_specs=pl.BlockSpec(memory_space=pltpu.VMEM),
        scratch_shapes=[
            pltpu.VMEM((SEQS, ROWS, HD), jnp.bfloat16),
            pltpu.VMEM((SEQS, count, HD), jnp.bfloat16),
            pltpu.VMEM((SEQS, count, HD), jnp.bfloat16),
            pltpu.VMEM((SEQS, ROWS, count), jnp.float32),
            pltpu.VMEM((SEQS, ROWS, HD), jnp.float32),
            pltpu.VMEM((SEQS, 2, ROWS, HD), jnp.float32),
            pltpu.SemaphoreType.DMA,
            pltpu.SemaphoreType.DMA((SEQS,)),
            pltpu.SemaphoreType.DMA((SEQS,)),
        ],
        compiler_params=pltpu.CompilerParams(vmem_limit_bytes=60 * MIB),
        name="attend",
    )(queries, keys, values)


def merge_kernel(last, parts_ref, out_ref):
    n = parts_ref.shape[0]
    maxima = parts_ref[:, MAX_ROW, :]
    highest = jnp.max(maxima, axis=0, keepdims=True)
    factors = jnp.exp2((maxima - highest) * SCALE_LOG2)
    total = jnp.sum(factors * parts_ref[:, TOTAL_ROW, :], axis=0, keepdims=True)
    by_row = jnp.transpose(jnp.concatenate([factors, jnp.broadcast_to(total, (8, HD))], axis=0))
    by_row = by_row[:BLOCK]
    merged = jnp.zeros((BLOCK, HD), jnp.float32)
    for i in range(n):
        merged = merged + parts_ref[i] * by_row[:, i : i + 1]
    row = lax.broadcasted_iota(jnp.int32, (BLOCK, HD), 0)
    if last:
        merged = jnp.where(row < PIECE, merged / by_row[:, n : n + 1], 0.0)
    else:
        merged = jnp.where(row < PIECE, merged, jnp.where(row == MAX_ROW, highest, total))
    for i in range(out_ref.shape[0]):
        out_ref[i] = merged


def merge(parts, copies, last):
    return pl.pallas_call(
        functools.partial(merge_kernel, last),
        out_shape=jax.ShapeDtypeStruct((copies, BLOCK, HD), jnp.float32),
        in_specs=[pl.BlockSpec(memory_space=pltpu.VMEM)],
        out_specs=pl.BlockSpec(memory_space=pltpu.VMEM),
        compiler_params=pltpu.CompilerParams(vmem_limit_bytes=4 * MIB),
        name="merge_last" if last else "merge",
    )(parts)


def finish_kernel(pieces_ref, out_ref):
    for s in range(SEQS):
        for q in range(QTOK):
            at = (s * QTOK + q) * (QH // PIECE)
            whole = [pieces_ref[at + i, 0:PIECE, :] for i in range(QH // PIECE)]
            out_ref[s, q] = jnp.concatenate(whole, axis=0).astype(jnp.bfloat16)


def finish(pieces):
    return pl.pallas_call(
        finish_kernel,
        out_shape=jax.ShapeDtypeStruct((SEQS, QTOK, QH, HD), jnp.bfloat16),
        in_specs=[pl.BlockSpec(memory_space=pltpu.VMEM)],
        out_specs=pl.BlockSpec(memory_space=pltpu.VMEM),
        compiler_params=pltpu.CompilerParams(vmem_limit_bytes=4 * MIB),
        name="finish",
    )(pieces)


def exchange(blocks, groups):
    return lax.all_to_all(blocks, AXES, 0, 0, tiled=True, axis_index_groups=groups)


def per_device(queries, keys, values):
    count = keys.shape[1] * KVH
    partials = attend(
        queries.reshape(SEQS, ROWS, HD),
        keys.reshape(SEQS, count, HD),
        values.reshape(SEQS, count, HD),
    )
    mine = merge(exchange(partials, SPREAD), len(HOLDERS[0]), False)
    done = merge(exchange(mine, HOLDERS), len(SPREAD[0]), True)
    return finish(exchange(done, SPREAD))


def solution(mesh):
    placed = (P(), P(None, AXES, None, None), P(None, AXES, None, None))
    return jax.shard_map(per_device, mesh=mesh, in_specs=placed, out_specs=P(), check_vma=False)
```

```python
import functools
import math

import jax
import jax.numpy as jnp
from jax import lax
from jax.experimental import pallas as pl
from jax.experimental.pallas import tpu as pltpu
from jax.sharding import PartitionSpec as P

QH = 40
KVH = 8
HD = 128
SEQS = 2
QTOK = 4
ROWS = QTOK * QH
PIECES = 32
PIECE = SEQS * ROWS // PIECES
SLABS, SLAB = 3, 4
DONE_SLABS, DONE_SLAB = 5, 2
SCALE_LOG2 = HD ** (-0.5) * math.log2(math.e)
CHUNK = 512
LOWEST = -1e30
AXES = ("gx", "gy")
MIB = 1 << 20


def device_index(core, x, y, z):
    return ((y * 2 + z // 4) * 2 + core) * 16 + x * 4 + z % 4


def planes(order):
    return [[device_index(core, x, y, z) for core, x, y in order] for z in range(8)]


SPREAD = planes([(core, x, y) for x in (2, 1, 0, 3) for y in (2, 1, 3, 0) for core in (1, 0)])
GATHER = planes([(core, x, y) for y in (2, 1, 0, 3) for x in (2, 1, 0, 3) for core in (1, 0)])
HOLDERS = [
    [device_index(core, x, y, z) for z in (4, 3, 5, 6, 0, 1, 7, 2)]
    for core in range(2)
    for x in range(4)
    for y in range(4)
]
PIECE_OF_SLOT = [SPREAD[0].index(device) for device in GATHER[0]]


def attend_kernel(q_hbm, k_hbm, v_hbm, out_ref, q_buf, k_buf, v_buf, scores, rows, stats, q_sem, k_sem, v_sem):
    count = k_buf.shape[1]
    q_copy = pltpu.make_async_copy(q_hbm, q_buf, q_sem)
    k_copy = [pltpu.make_async_copy(k_hbm.at[s], k_buf.at[s], k_sem.at[s]) for s in range(SEQS)]
    v_copy = [pltpu.make_async_copy(v_hbm.at[s], v_buf.at[s], v_sem.at[s]) for s in range(SEQS)]
    q_copy.start()
    for s in range(SEQS):
        k_copy[s].start()
        v_copy[s].start()
    row = lax.broadcasted_iota(jnp.int32, (ROWS, HD), 0)
    lane = lax.broadcasted_iota(jnp.int32, (ROWS, HD), 1)
    own_head = (row % QH) // (QH // KVH) == lane % KVH
    bias = jnp.where(own_head, 0.0, LOWEST).astype(jnp.float32)
    diagonal = row % PIECE == lane
    zero = jnp.zeros((ROWS, HD), jnp.float32)

    def score(s, j, highest):
        part = lax.dot_general(
            q_buf[s],
            k_buf[s, pl.ds(j, CHUNK), :],
            (((1,), (1,)), ((), ())),
            preferred_element_type=jnp.float32,
        )
        for i in range(0, CHUNK, HD):
            own = part[:, i : i + HD] + bias
            scores[s, :, pl.ds(j + i, HD)] = own
            highest = jnp.maximum(highest, own)
        return highest

    def weigh(s, j, block_max, total, block_out):
        weights = jnp.exp2((scores[s, :, pl.ds(j, CHUNK)] - block_max) * SCALE_LOG2)
        for i in range(0, CHUNK, HD):
            total = total + weights[:, i : i + HD]
        block_out = block_out + jnp.dot(
            weights.astype(jnp.bfloat16),
            v_buf[s, pl.ds(j, CHUNK), :],
            preferred_element_type=jnp.float32,
        )
        return total, block_out

    def write(s, block_max, total, block_out):
        rows[s] = block_out
        stats[s, 0] = jnp.where(diagonal, block_max, 0.0)
        stats[s, 1] = jnp.where(diagonal, jnp.sum(total, axis=1, keepdims=True), 0.0)
        for p in range(ROWS // PIECE):
            at = s * (ROWS // PIECE) + p
            for r in range(0, PIECE, SLAB):
                n = min(SLAB, PIECE - r)
                out_ref[at, r // SLAB, 0:n, :] = rows[s, pl.ds(p * PIECE + r, n), :]
            own = pl.ds(p * PIECE, PIECE)
            for i in range(2):
                out_ref[at, SLABS - 1, SLAB - 2 + i : SLAB - 1 + i, :] = jnp.sum(stats[s, i, own, :], axis=0, keepdims=True)

    q_copy.wait()
    k_copy[0].wait()
    highest = jnp.full((ROWS, HD), LOWEST, jnp.float32)
    for j in range(0, count, CHUNK):
        highest = score(0, j, highest)
    block_max = jnp.max(highest, axis=1, keepdims=True)
    for s in range(SEQS):
        if s + 1 < SEQS:
            k_copy[s + 1].wait()
        v_copy[s].wait()
        highest = jnp.full((ROWS, HD), LOWEST, jnp.float32)
        total, block_out = zero, zero
        for j in range(0, count, CHUNK):
            if s + 1 < SEQS:
                highest = score(s + 1, j, highest)
            total, block_out = weigh(s, j, block_max, total, block_out)
        write(s, block_max, total, block_out)
        block_max = jnp.max(highest, axis=1, keepdims=True)


def attend(queries, keys, values):
    count = keys.shape[1]
    return pl.pallas_call(
        attend_kernel,
        out_shape=jax.ShapeDtypeStruct((PIECES, SLABS, SLAB, HD), jnp.float32),
        in_specs=[pl.BlockSpec(memory_space=pltpu.HBM)] * 3,
        out_specs=pl.BlockSpec(memory_space=pltpu.VMEM),
        scratch_shapes=[
            pltpu.VMEM((SEQS, ROWS, HD), jnp.bfloat16),
            pltpu.VMEM((SEQS, count, HD), jnp.bfloat16),
            pltpu.VMEM((SEQS, count, HD), jnp.bfloat16),
            pltpu.VMEM((SEQS, ROWS, count), jnp.float32),
            pltpu.VMEM((SEQS, ROWS, HD), jnp.float32),
            pltpu.VMEM((SEQS, 2, ROWS, HD), jnp.float32),
            pltpu.SemaphoreType.DMA,
            pltpu.SemaphoreType.DMA((SEQS,)),
            pltpu.SemaphoreType.DMA((SEQS,)),
        ],
        compiler_params=pltpu.CompilerParams(vmem_limit_bytes=32 * MIB),
        name="attend",
    )(*(pltpu.with_memory_space_constraint(array, pltpu.HBM) for array in (queries, keys, values)))


def merge_kernel(last, parts_ref, out_ref):
    n = parts_ref.shape[0]
    maxima = parts_ref[:, SLABS - 1, SLAB - 2, :]
    highest = jnp.max(maxima, axis=0, keepdims=True)
    factors = jnp.exp2((maxima - highest) * SCALE_LOG2)
    total = jnp.sum(factors * parts_ref[:, SLABS - 1, SLAB - 1, :], axis=0, keepdims=True)
    by_row = jnp.transpose(jnp.concatenate([factors, jnp.broadcast_to(total, (8, HD))], axis=0))
    for a in range(SLABS):
        factor = by_row[a * SLAB : (a + 1) * SLAB]
        merged = jnp.zeros((SLAB, HD), jnp.float32)
        for i in range(n):
            merged = merged + parts_ref[i, a] * factor[:, i : i + 1]
        if last:
            merged = merged / factor[:, n : n + 1]
            for r in range(0, min(SLAB, PIECE - a * SLAB), DONE_SLAB):
                done = merged[r : r + DONE_SLAB]
                for i in range(out_ref.shape[0]):
                    out_ref[i, (a * SLAB + r) // DONE_SLAB] = done
        else:
            row = lax.broadcasted_iota(jnp.int32, (SLAB, HD), 0) + a * SLAB
            merged = jnp.where(row < PIECE, merged, jnp.where(row == PIECE, highest, total))
            for i in range(out_ref.shape[0]):
                out_ref[i, a] = merged


def merge(parts, copies, last):
    block = (DONE_SLABS, DONE_SLAB) if last else (SLABS, SLAB)
    return pl.pallas_call(
        functools.partial(merge_kernel, last),
        out_shape=jax.ShapeDtypeStruct((copies, *block, HD), jnp.float32),
        in_specs=[pl.BlockSpec(memory_space=pltpu.VMEM)],
        out_specs=pl.BlockSpec(memory_space=pltpu.VMEM),
        compiler_params=pltpu.CompilerParams(vmem_limit_bytes=4 * MIB),
        name="merge_last" if last else "merge",
    )(parts)


def finish_kernel(pieces_ref, out_ref, rows):
    for slot, piece in enumerate(PIECE_OF_SLOT):
        for a in range(DONE_SLABS):
            rows[pl.ds(piece * PIECE + a * DONE_SLAB, DONE_SLAB), :] = pieces_ref[slot, a]
    for s in range(SEQS):
        for q in range(QTOK):
            out_ref[s, q] = rows[pl.ds((s * QTOK + q) * QH, QH), :].astype(jnp.bfloat16)


def finish(pieces):
    return pl.pallas_call(
        finish_kernel,
        out_shape=jax.ShapeDtypeStruct((SEQS, QTOK, QH, HD), jnp.bfloat16),
        in_specs=[pl.BlockSpec(memory_space=pltpu.VMEM)],
        out_specs=pl.BlockSpec(memory_space=pltpu.VMEM),
        scratch_shapes=[pltpu.VMEM((SEQS * ROWS, HD), jnp.float32)],
        compiler_params=pltpu.CompilerParams(vmem_limit_bytes=4 * MIB),
        name="finish",
    )(pieces)


def exchange(blocks, groups):
    return lax.all_to_all(blocks, AXES, 0, 0, tiled=True, axis_index_groups=groups)


def per_device(queries, keys, values):
    count = keys.shape[1] * KVH
    partials = attend(
        queries.reshape(SEQS, ROWS, HD),
        keys.reshape(SEQS, count, HD),
        values.reshape(SEQS, count, HD),
    )
    mine = merge(exchange(partials, SPREAD), len(HOLDERS[0]), False)
    done = merge(exchange(mine, HOLDERS), len(GATHER[0]), True)
    return finish(exchange(done, GATHER))


def solution(mesh):
    placed = (P(), P(None, AXES, None, None), P(None, AXES, None, None))
    return jax.shard_map(per_device, mesh=mesh, in_specs=placed, out_specs=P(), check_vma=False)
```

```python
import functools
import math

import jax
import jax.numpy as jnp
from jax import lax
from jax.experimental import pallas as pl
from jax.experimental.pallas import tpu as pltpu
from jax.sharding import PartitionSpec as P

QH = 40
KVH = 8
HD = 128
SEQS = 2
QTOK = 4
ROWS = QTOK * QH
PIECES = 32
PIECE = SEQS * ROWS // PIECES
SLABS, SLAB = 3, 4
DONE_SLABS, DONE_SLAB = 5, 2
SCALE_LOG2 = HD ** (-0.5) * math.log2(math.e)
CHUNK = 512
LOWEST = -1e30
AXES = ("gx", "gy")
MIB = 1 << 20


def device_index(core, x, y, z):
    return ((y * 2 + z // 4) * 2 + core) * 16 + x * 4 + z % 4


def planes(order):
    return [[device_index(core, x, y, z) for core, x, y in order] for z in range(8)]


SPREAD = planes([(core, x, y) for x in (2, 1, 0, 3) for y in (2, 1, 3, 0) for core in (1, 0)])
GATHER = planes([(core, x, y) for y in (2, 1, 0, 3) for x in (2, 1, 0, 3) for core in (1, 0)])
HOLDERS = [
    [device_index(core, x, y, z) for z in (4, 3, 5, 6, 0, 1, 7, 2)]
    for core in range(2)
    for x in range(4)
    for y in range(4)
]
PIECE_OF_SLOT = [SPREAD[0].index(device) for device in GATHER[0]]


def attend_kernel(q_hbm, k_hbm, v_hbm, out_ref, q_buf, k_buf, v_buf, scores, rows, stats, q_sem, k_sem, v_sem):
    count = k_buf.shape[1]
    q_copy = pltpu.make_async_copy(q_hbm, q_buf, q_sem)
    k_copy = [pltpu.make_async_copy(k_hbm.at[s], k_buf.at[s], k_sem.at[s]) for s in range(SEQS)]
    v_copy = [pltpu.make_async_copy(v_hbm.at[s], v_buf.at[s], v_sem.at[s]) for s in range(SEQS)]
    q_copy.start()
    for s in range(SEQS):
        k_copy[s].start(priority=0)
        v_copy[s].start(priority=1)
    row = lax.broadcasted_iota(jnp.int32, (ROWS, HD), 0)
    lane = lax.broadcasted_iota(jnp.int32, (ROWS, HD), 1)
    own_head = (row % QH) // (QH // KVH) == lane % KVH
    bias = jnp.where(own_head, 0.0, LOWEST).astype(jnp.float32)
    diagonal = row % PIECE == lane
    zero = jnp.zeros((ROWS, HD), jnp.float32)

    def score(s, j, highest):
        part = lax.dot_general(
            q_buf[s],
            k_buf[s, pl.ds(j, CHUNK), :],
            (((1,), (1,)), ((), ())),
            preferred_element_type=jnp.float32,
        )
        for i in range(0, CHUNK, HD):
            own = part[:, i : i + HD] + bias
            scores[s, :, pl.ds(j + i, HD)] = own
            highest = jnp.maximum(highest, own)
        return highest

    def weigh(s, j, block_max, total, block_out):
        weights = jnp.exp2((scores[s, :, pl.ds(j, CHUNK)] - block_max) * SCALE_LOG2)
        for i in range(0, CHUNK, HD):
            total = total + weights[:, i : i + HD]
        block_out = block_out + jnp.dot(
            weights.astype(jnp.bfloat16),
            v_buf[s, pl.ds(j, CHUNK), :],
            preferred_element_type=jnp.float32,
        )
        return total, block_out

    def write(s, block_max, total, block_out):
        rows[s] = block_out
        stats[s, 0] = jnp.where(diagonal, block_max, 0.0)
        stats[s, 1] = jnp.where(diagonal, jnp.sum(total, axis=1, keepdims=True), 0.0)
        for p in range(ROWS // PIECE):
            at = s * (ROWS // PIECE) + p
            for r in range(0, PIECE, SLAB):
                n = min(SLAB, PIECE - r)
                out_ref[at, r // SLAB, 0:n, :] = rows[s, pl.ds(p * PIECE + r, n), :]
            own = pl.ds(p * PIECE, PIECE)
            for i in range(2):
                out_ref[at, SLABS - 1, SLAB - 2 + i : SLAB - 1 + i, :] = jnp.sum(stats[s, i, own, :], axis=0, keepdims=True)

    q_copy.wait()
    k_copy[0].wait()
    highest = jnp.full((ROWS, HD), LOWEST, jnp.float32)
    for j in range(0, count, CHUNK):
        highest = score(0, j, highest)
    block_max = jnp.max(highest, axis=1, keepdims=True)
    for s in range(SEQS):
        if s + 1 < SEQS:
            k_copy[s + 1].wait()
        v_copy[s].wait()
        highest = jnp.full((ROWS, HD), LOWEST, jnp.float32)
        total, block_out = zero, zero
        for j in range(0, count, CHUNK):
            if s + 1 < SEQS:
                highest = score(s + 1, j, highest)
            total, block_out = weigh(s, j, block_max, total, block_out)
        write(s, block_max, total, block_out)
        block_max = jnp.max(highest, axis=1, keepdims=True)


def attend(queries, keys, values):
    count = keys.shape[1]
    return pl.pallas_call(
        attend_kernel,
        out_shape=jax.ShapeDtypeStruct((PIECES, SLABS, SLAB, HD), jnp.float32),
        in_specs=[pl.BlockSpec(memory_space=pltpu.HBM)] * 3,
        out_specs=pl.BlockSpec(memory_space=pltpu.VMEM),
        scratch_shapes=[
            pltpu.VMEM((SEQS, ROWS, HD), jnp.bfloat16),
            pltpu.VMEM((SEQS, count, HD), jnp.bfloat16),
            pltpu.VMEM((SEQS, count, HD), jnp.bfloat16),
            pltpu.VMEM((SEQS, ROWS, count), jnp.float32),
            pltpu.VMEM((SEQS, ROWS, HD), jnp.float32),
            pltpu.VMEM((SEQS, 2, ROWS, HD), jnp.float32),
            pltpu.SemaphoreType.DMA,
            pltpu.SemaphoreType.DMA((SEQS,)),
            pltpu.SemaphoreType.DMA((SEQS,)),
        ],
        compiler_params=pltpu.CompilerParams(vmem_limit_bytes=32 * MIB),
        name="attend",
    )(*(pltpu.with_memory_space_constraint(array, pltpu.HBM) for array in (queries, keys, values)))


def merge_kernel(last, parts_ref, out_ref):
    n = parts_ref.shape[0]
    maxima = parts_ref[:, SLABS - 1, SLAB - 2, :]
    highest = jnp.max(maxima, axis=0, keepdims=True)
    factors = jnp.exp2((maxima - highest) * SCALE_LOG2)
    total = jnp.sum(factors * parts_ref[:, SLABS - 1, SLAB - 1, :], axis=0, keepdims=True)
    by_row = jnp.transpose(jnp.concatenate([factors, jnp.broadcast_to(total, (8, HD))], axis=0))
    for a in range(SLABS):
        factor = by_row[a * SLAB : (a + 1) * SLAB]
        merged = jnp.zeros((SLAB, HD), jnp.float32)
        for i in range(n):
            merged = merged + parts_ref[i, a] * factor[:, i : i + 1]
        if last:
            merged = merged / factor[:, n : n + 1]
            for r in range(0, min(SLAB, PIECE - a * SLAB), DONE_SLAB):
                done = merged[r : r + DONE_SLAB]
                for i in range(out_ref.shape[0]):
                    out_ref[i, (a * SLAB + r) // DONE_SLAB] = done
        else:
            row = lax.broadcasted_iota(jnp.int32, (SLAB, HD), 0) + a * SLAB
            merged = jnp.where(row < PIECE, merged, jnp.where(row == PIECE, highest, total))
            for i in range(out_ref.shape[0]):
                out_ref[i, a] = merged


def merge(parts, copies, last):
    block = (DONE_SLABS, DONE_SLAB) if last else (SLABS, SLAB)
    return pl.pallas_call(
        functools.partial(merge_kernel, last),
        out_shape=jax.ShapeDtypeStruct((copies, *block, HD), jnp.float32),
        in_specs=[pl.BlockSpec(memory_space=pltpu.VMEM)],
        out_specs=pl.BlockSpec(memory_space=pltpu.VMEM),
        compiler_params=pltpu.CompilerParams(vmem_limit_bytes=4 * MIB),
        name="merge_last" if last else "merge",
    )(parts)


def finish_kernel(pieces_ref, out_ref, rows):
    for slot, piece in enumerate(PIECE_OF_SLOT):
        for a in range(DONE_SLABS):
            rows[pl.ds(piece * PIECE + a * DONE_SLAB, DONE_SLAB), :] = pieces_ref[slot, a]
    for s in range(SEQS):
        for q in range(QTOK):
            out_ref[s, q] = rows[pl.ds((s * QTOK + q) * QH, QH), :].astype(jnp.bfloat16)


def finish(pieces):
    return pl.pallas_call(
        finish_kernel,
        out_shape=jax.ShapeDtypeStruct((SEQS, QTOK, QH, HD), jnp.bfloat16),
        in_specs=[pl.BlockSpec(memory_space=pltpu.VMEM)],
        out_specs=pl.BlockSpec(memory_space=pltpu.VMEM),
        scratch_shapes=[pltpu.VMEM((SEQS * ROWS, HD), jnp.float32)],
        compiler_params=pltpu.CompilerParams(vmem_limit_bytes=4 * MIB),
        name="finish",
    )(pieces)


def exchange(blocks, groups):
    return lax.all_to_all(blocks, AXES, 0, 0, tiled=True, axis_index_groups=groups)


def per_device(queries, keys, values):
    count = keys.shape[1] * KVH
    partials = attend(
        queries.reshape(SEQS, ROWS, HD),
        keys.reshape(SEQS, count, HD),
        values.reshape(SEQS, count, HD),
    )
    mine = merge(exchange(partials, SPREAD), len(HOLDERS[0]), False)
    done = merge(exchange(mine, HOLDERS), len(GATHER[0]), True)
    return finish(exchange(done, GATHER))


def solution(mesh):
    placed = (P(), P(None, AXES, None, None), P(None, AXES, None, None))
    return jax.shard_map(per_device, mesh=mesh, in_specs=placed, out_specs=P(), check_vma=False)
```

```python
import functools
import math

import jax
import jax.numpy as jnp
from jax import lax
from jax.experimental import pallas as pl
from jax.experimental.pallas import tpu as pltpu
from jax.sharding import PartitionSpec as P

QH = 40
KVH = 8
HD = 128
SEQS = 2
QTOK = 4
ROWS = QTOK * QH
PIECES = 32
PIECE = SEQS * ROWS // PIECES
SLABS, SLAB = 3, 4
DONE_SLABS, DONE_SLAB = 5, 2
SCALE_LOG2 = HD ** (-0.5) * math.log2(math.e)
CHUNK = 512
LOWEST = -1e30
AXES = ("gx", "gy")
MIB = 1 << 20


def device_index(core, x, y, z):
    return ((y * 2 + z // 4) * 2 + core) * 16 + x * 4 + z % 4


def planes(order):
    return [[device_index(core, x, y, z) for core, x, y in order] for z in range(8)]


SPREAD = planes([(core, x, y) for x in (2, 1, 0, 3) for y in (2, 1, 3, 0) for core in (1, 0)])
GATHER = planes([(core, x, y) for y in (2, 1, 0, 3) for x in (2, 1, 0, 3) for core in (1, 0)])
HOLDERS = [
    [device_index(core, x, y, z) for z in (4, 3, 5, 6, 0, 1, 7, 2)]
    for core in range(2)
    for x in range(4)
    for y in range(4)
]
PIECE_OF_SLOT = [SPREAD[0].index(device) for device in GATHER[0]]


def attend_kernel(q_hbm, k_hbm, v_hbm, out_ref, q_buf, k_buf, v_buf, scores, rows, stats, q_sem, k_sem, v_sem):
    count = k_buf.shape[1]
    q_copy = pltpu.make_async_copy(q_hbm, q_buf, q_sem)
    k_copy = [pltpu.make_async_copy(k_hbm.at[s], k_buf.at[s], k_sem.at[s]) for s in range(SEQS)]
    v_copy = [pltpu.make_async_copy(v_hbm.at[s], v_buf.at[s], v_sem.at[s]) for s in range(SEQS)]
    q_copy.start()
    for s in range(SEQS):
        k_copy[s].start(priority=0)
        v_copy[s].start(priority=1)
    row = lax.broadcasted_iota(jnp.int32, (ROWS, HD), 0)
    lane = lax.broadcasted_iota(jnp.int32, (ROWS, HD), 1)
    own_head = (row % QH) // (QH // KVH) == lane % KVH
    bias = jnp.where(own_head, 0.0, LOWEST).astype(jnp.float32)
    diagonal = row % PIECE == lane
    zero = jnp.zeros((ROWS, HD), jnp.float32)

    def score(s, j, highest):
        part = lax.dot_general(
            q_buf[s],
            k_buf[s, pl.ds(j, CHUNK), :],
            (((1,), (1,)), ((), ())),
            preferred_element_type=jnp.float32,
        )
        for i in range(0, CHUNK, HD):
            own = part[:, i : i + HD] * SCALE_LOG2 + bias
            scores[s, :, pl.ds(j + i, HD)] = own
            highest = jnp.maximum(highest, own)
        return highest

    def weigh(s, j, block_max, total, block_out):
        weights = jnp.exp2(scores[s, :, pl.ds(j, CHUNK)] - block_max)
        for i in range(0, CHUNK, HD):
            total = total + weights[:, i : i + HD]
        block_out = block_out + jnp.dot(
            weights.astype(jnp.bfloat16),
            v_buf[s, pl.ds(j, CHUNK), :],
            preferred_element_type=jnp.float32,
        )
        return total, block_out

    def write(s, block_max, total, block_out):
        rows[s] = block_out
        stats[s, 0] = jnp.where(diagonal, block_max, 0.0)
        stats[s, 1] = jnp.where(diagonal, jnp.sum(total, axis=1, keepdims=True), 0.0)
        for p in range(ROWS // PIECE):
            at = s * (ROWS // PIECE) + p
            for r in range(0, PIECE, SLAB):
                n = min(SLAB, PIECE - r)
                out_ref[at, r // SLAB, 0:n, :] = rows[s, pl.ds(p * PIECE + r, n), :]
            own = pl.ds(p * PIECE, PIECE)
            for i in range(2):
                out_ref[at, SLABS - 1, SLAB - 2 + i : SLAB - 1 + i, :] = jnp.sum(stats[s, i, own, :], axis=0, keepdims=True)

    q_copy.wait()
    k_copy[0].wait()
    highest = jnp.full((ROWS, HD), LOWEST, jnp.float32)
    for j in range(0, count, CHUNK):
        highest = score(0, j, highest)
    block_max = jnp.max(highest, axis=1, keepdims=True)
    for s in range(SEQS):
        if s + 1 < SEQS:
            k_copy[s + 1].wait()
        v_copy[s].wait()
        highest = jnp.full((ROWS, HD), LOWEST, jnp.float32)
        total, block_out = zero, zero
        for j in range(0, count, CHUNK):
            if s + 1 < SEQS:
                highest = score(s + 1, j, highest)
            total, block_out = weigh(s, j, block_max, total, block_out)
        write(s, block_max, total, block_out)
        block_max = jnp.max(highest, axis=1, keepdims=True)


def attend(queries, keys, values):
    count = keys.shape[1]
    return pl.pallas_call(
        attend_kernel,
        out_shape=jax.ShapeDtypeStruct((PIECES, SLABS, SLAB, HD), jnp.float32),
        in_specs=[pl.BlockSpec(memory_space=pltpu.HBM)] * 3,
        out_specs=pl.BlockSpec(memory_space=pltpu.VMEM),
        scratch_shapes=[
            pltpu.VMEM((SEQS, ROWS, HD), jnp.bfloat16),
            pltpu.VMEM((SEQS, count, HD), jnp.bfloat16),
            pltpu.VMEM((SEQS, count, HD), jnp.bfloat16),
            pltpu.VMEM((SEQS, ROWS, count), jnp.float32),
            pltpu.VMEM((SEQS, ROWS, HD), jnp.float32),
            pltpu.VMEM((SEQS, 2, ROWS, HD), jnp.float32),
            pltpu.SemaphoreType.DMA,
            pltpu.SemaphoreType.DMA((SEQS,)),
            pltpu.SemaphoreType.DMA((SEQS,)),
        ],
        compiler_params=pltpu.CompilerParams(vmem_limit_bytes=32 * MIB),
        name="attend",
    )(*(pltpu.with_memory_space_constraint(array, pltpu.HBM) for array in (queries, keys, values)))


def merge_kernel(last, parts_ref, out_ref):
    n = parts_ref.shape[0]
    maxima = parts_ref[:, SLABS - 1, SLAB - 2, :]
    highest = jnp.max(maxima, axis=0, keepdims=True)
    factors = jnp.exp2(maxima - highest)
    total = jnp.sum(factors * parts_ref[:, SLABS - 1, SLAB - 1, :], axis=0, keepdims=True)
    by_row = jnp.transpose(jnp.concatenate([factors, jnp.broadcast_to(total, (8, HD))], axis=0))
    for a in range(SLABS):
        factor = by_row[a * SLAB : (a + 1) * SLAB]
        merged = jnp.zeros((SLAB, HD), jnp.float32)
        for i in range(n):
            merged = merged + parts_ref[i, a] * factor[:, i : i + 1]
        if last:
            merged = merged / factor[:, n : n + 1]
            for r in range(0, min(SLAB, PIECE - a * SLAB), DONE_SLAB):
                done = merged[r : r + DONE_SLAB]
                for i in range(out_ref.shape[0]):
                    out_ref[i, (a * SLAB + r) // DONE_SLAB] = done
        else:
            row = lax.broadcasted_iota(jnp.int32, (SLAB, HD), 0) + a * SLAB
            merged = jnp.where(row < PIECE, merged, jnp.where(row == PIECE, highest, total))
            for i in range(out_ref.shape[0]):
                out_ref[i, a] = merged


def merge(parts, copies, last):
    block = (DONE_SLABS, DONE_SLAB) if last else (SLABS, SLAB)
    return pl.pallas_call(
        functools.partial(merge_kernel, last),
        out_shape=jax.ShapeDtypeStruct((copies, *block, HD), jnp.float32),
        in_specs=[pl.BlockSpec(memory_space=pltpu.VMEM)],
        out_specs=pl.BlockSpec(memory_space=pltpu.VMEM),
        compiler_params=pltpu.CompilerParams(vmem_limit_bytes=4 * MIB),
        name="merge_last" if last else "merge",
    )(parts)


def finish_kernel(pieces_ref, out_ref, rows):
    for slot, piece in enumerate(PIECE_OF_SLOT):
        for a in range(DONE_SLABS):
            rows[pl.ds(piece * PIECE + a * DONE_SLAB, DONE_SLAB), :] = pieces_ref[slot, a]
    for s in range(SEQS):
        for q in range(QTOK):
            out_ref[s, q] = rows[pl.ds((s * QTOK + q) * QH, QH), :].astype(jnp.bfloat16)


def finish(pieces):
    return pl.pallas_call(
        finish_kernel,
        out_shape=jax.ShapeDtypeStruct((SEQS, QTOK, QH, HD), jnp.bfloat16),
        in_specs=[pl.BlockSpec(memory_space=pltpu.VMEM)],
        out_specs=pl.BlockSpec(memory_space=pltpu.VMEM),
        scratch_shapes=[pltpu.VMEM((SEQS * ROWS, HD), jnp.float32)],
        compiler_params=pltpu.CompilerParams(vmem_limit_bytes=4 * MIB),
        name="finish",
    )(pieces)


def exchange(blocks, groups):
    return lax.all_to_all(blocks, AXES, 0, 0, tiled=True, axis_index_groups=groups)


def per_device(queries, keys, values):
    count = keys.shape[1] * KVH
    partials = attend(
        queries.reshape(SEQS, ROWS, HD),
        keys.reshape(SEQS, count, HD),
        values.reshape(SEQS, count, HD),
    )
    mine = merge(exchange(partials, SPREAD), len(HOLDERS[0]), False)
    done = merge(exchange(mine, HOLDERS), len(GATHER[0]), True)
    return finish(exchange(done, GATHER))


def solution(mesh):
    placed = (P(), P(None, AXES, None, None), P(None, AXES, None, None))
    return jax.shard_map(per_device, mesh=mesh, in_specs=placed, out_specs=P(), check_vma=False)
```

```python
import functools
import math

import jax
import jax.numpy as jnp
from jax import lax
from jax.experimental import pallas as pl
from jax.experimental.pallas import tpu as pltpu
from jax.sharding import PartitionSpec as P

QH = 40
KVH = 8
HD = 128
SEQS = 2
QTOK = 4
ROWS = QTOK * QH
PIECES = 32
PIECE = SEQS * ROWS // PIECES
SLABS, SLAB = 3, 4
DONE_SLABS, DONE_SLAB = 5, 2
SCALE_LOG2 = HD ** (-0.5) * math.log2(math.e)
CHUNK = 512
LOWEST = -1e30
AXES = ("gx", "gy")
MIB = 1 << 20


def device_index(core, x, y, z):
    return ((y * 2 + z // 4) * 2 + core) * 16 + x * 4 + z % 4


def planes(order):
    return [[device_index(core, x, y, z) for core, x, y in order] for z in range(8)]


SPREAD = planes([(core, x, y) for x in (2, 1, 0, 3) for y in (2, 1, 3, 0) for core in (1, 0)])
GATHER = planes([(core, x, y) for y in (2, 1, 0, 3) for x in (2, 1, 0, 3) for core in (1, 0)])
HOLDERS = [
    [device_index(core, x, y, z) for z in (4, 3, 5, 6, 0, 1, 7, 2)]
    for core in range(2)
    for x in range(4)
    for y in range(4)
]
PIECE_OF_SLOT = [SPREAD[0].index(device) for device in GATHER[0]]


def attend_kernel(q_hbm, k_hbm, v_hbm, out_ref, q_buf, k_buf, v_buf, scores, rows, stats, q_sem, k_sem, v_sem):
    count = k_buf.shape[1]
    q_copy = pltpu.make_async_copy(q_hbm, q_buf, q_sem)
    k_copy = [pltpu.make_async_copy(k_hbm.at[s], k_buf.at[s], k_sem.at[s]) for s in range(SEQS)]
    v_copy = [pltpu.make_async_copy(v_hbm.at[s], v_buf.at[s], v_sem.at[s]) for s in range(SEQS)]
    q_copy.start()
    for s in range(SEQS):
        k_copy[s].start(priority=0)
        v_copy[s].start(priority=1)
    row = lax.broadcasted_iota(jnp.int32, (ROWS, HD), 0)
    lane = lax.broadcasted_iota(jnp.int32, (ROWS, HD), 1)
    own_head = (row % QH) // (QH // KVH) == lane % KVH
    bias = jnp.where(own_head, 0.0, LOWEST).astype(jnp.float32)
    diagonal = row % PIECE == lane
    zero = jnp.zeros((ROWS, HD), jnp.float32)

    def score(s, j, highest):
        part = lax.dot_general(
            q_buf[s],
            k_buf[s, pl.ds(j, CHUNK), :],
            (((1,), (1,)), ((), ())),
            preferred_element_type=jnp.float32,
        )
        for i in range(0, CHUNK, HD):
            own = part[:, i : i + HD] + bias
            scores[s, :, pl.ds(j + i, HD)] = own
            highest = jnp.maximum(highest, own)
        return highest

    def weigh(s, j, block_max, total, block_out):
        weights = jnp.exp2((scores[s, :, pl.ds(j, CHUNK)] - block_max) * SCALE_LOG2)
        for i in range(0, CHUNK, HD):
            total = total + weights[:, i : i + HD]
        block_out = block_out + jnp.dot(
            weights.astype(jnp.bfloat16),
            v_buf[s, pl.ds(j, CHUNK), :],
            preferred_element_type=jnp.float32,
        )
        return total, block_out

    def write(s, block_max, total, block_out):
        rows[s] = block_out
        stats[s, 0] = jnp.where(diagonal, block_max, 0.0)
        stats[s, 1] = jnp.where(diagonal, jnp.sum(total, axis=1, keepdims=True), 0.0)
        for p in range(ROWS // PIECE):
            at = s * (ROWS // PIECE) + p
            for r in range(0, PIECE, SLAB):
                n = min(SLAB, PIECE - r)
                out_ref[at, r // SLAB, 0:n, :] = rows[s, pl.ds(p * PIECE + r, n), :]
            own = pl.ds(p * PIECE, PIECE)
            for i in range(2):
                out_ref[at, SLABS - 1, SLAB - 2 + i : SLAB - 1 + i, :] = jnp.sum(stats[s, i, own, :], axis=0, keepdims=True)

    q_copy.wait()
    k_copy[0].wait()
    highest = jnp.full((ROWS, HD), LOWEST, jnp.float32)
    for j in range(0, count, CHUNK):
        highest = score(0, j, highest)
    block_max = jnp.max(highest, axis=1, keepdims=True)
    for s in range(SEQS):
        if s + 1 < SEQS:
            k_copy[s + 1].wait()
        v_copy[s].wait()
        highest = jnp.full((ROWS, HD), LOWEST, jnp.float32)
        total, block_out = zero, zero
        for j in range(0, count, CHUNK):
            if s + 1 < SEQS:
                highest = score(s + 1, j, highest)
            total, block_out = weigh(s, j, block_max, total, block_out)
        write(s, block_max, total, block_out)
        block_max = jnp.max(highest, axis=1, keepdims=True)


def attend(queries, keys, values):
    count = keys.shape[1]
    return pl.pallas_call(
        attend_kernel,
        out_shape=jax.ShapeDtypeStruct((PIECES, SLABS, SLAB, HD), jnp.float32),
        in_specs=[pl.BlockSpec(memory_space=pltpu.HBM)] * 3,
        out_specs=pl.BlockSpec(memory_space=pltpu.VMEM),
        scratch_shapes=[
            pltpu.VMEM((SEQS, ROWS, HD), jnp.bfloat16),
            pltpu.VMEM((SEQS, count, HD), jnp.bfloat16),
            pltpu.VMEM((SEQS, count, HD), jnp.bfloat16),
            pltpu.VMEM((SEQS, ROWS, count), jnp.float32),
            pltpu.VMEM((SEQS, ROWS, HD), jnp.float32),
            pltpu.VMEM((SEQS, 2, ROWS, HD), jnp.float32),
            pltpu.SemaphoreType.DMA,
            pltpu.SemaphoreType.DMA((SEQS,)),
            pltpu.SemaphoreType.DMA((SEQS,)),
        ],
        compiler_params=pltpu.CompilerParams(vmem_limit_bytes=32 * MIB),
        name="attend",
    )(*(pltpu.with_memory_space_constraint(array, pltpu.HBM) for array in (queries, keys, values)))


def merge_kernel(last, parts_ref, out_ref):
    maxima = parts_ref[:, SLABS - 1, SLAB - 2, :]
    highest = jnp.max(maxima, axis=0, keepdims=True)
    factors = jnp.exp2((maxima - highest) * SCALE_LOG2)
    total = jnp.sum(factors * parts_ref[:, SLABS - 1, SLAB - 1, :], axis=0, keepdims=True)
    merged = []
    for r in range(PIECE):
        own = jnp.sum(parts_ref[:, r // SLAB, r % SLAB, :] * factors[:, r : r + 1], axis=0, keepdims=True)
        merged.append(own / total[:, r : r + 1] if last else own)
    slab = DONE_SLAB if last else SLAB
    merged += [] if last else [highest, total]
    for a in range(len(merged) // slab):
        rows = jnp.concatenate(merged[a * slab : (a + 1) * slab], axis=0)
        for i in range(out_ref.shape[0]):
            out_ref[i, a] = rows


def merge(parts, copies, last):
    block = (DONE_SLABS, DONE_SLAB) if last else (SLABS, SLAB)
    return pl.pallas_call(
        functools.partial(merge_kernel, last),
        out_shape=jax.ShapeDtypeStruct((copies, *block, HD), jnp.float32),
        in_specs=[pl.BlockSpec(memory_space=pltpu.VMEM)],
        out_specs=pl.BlockSpec(memory_space=pltpu.VMEM),
        compiler_params=pltpu.CompilerParams(vmem_limit_bytes=4 * MIB),
        name="merge_last" if last else "merge",
    )(parts)


def finish_kernel(pieces_ref, out_ref, rows):
    for slot, piece in enumerate(PIECE_OF_SLOT):
        for a in range(DONE_SLABS):
            rows[pl.ds(piece * PIECE + a * DONE_SLAB, DONE_SLAB), :] = pieces_ref[slot, a]
    for s in range(SEQS):
        for q in range(QTOK):
            out_ref[s, q] = rows[pl.ds((s * QTOK + q) * QH, QH), :].astype(jnp.bfloat16)


def finish(pieces):
    return pl.pallas_call(
        finish_kernel,
        out_shape=jax.ShapeDtypeStruct((SEQS, QTOK, QH, HD), jnp.bfloat16),
        in_specs=[pl.BlockSpec(memory_space=pltpu.VMEM)],
        out_specs=pl.BlockSpec(memory_space=pltpu.VMEM),
        scratch_shapes=[pltpu.VMEM((SEQS * ROWS, HD), jnp.float32)],
        compiler_params=pltpu.CompilerParams(vmem_limit_bytes=4 * MIB),
        name="finish",
    )(pieces)


def exchange(blocks, groups):
    return lax.all_to_all(blocks, AXES, 0, 0, tiled=True, axis_index_groups=groups)


def per_device(queries, keys, values):
    count = keys.shape[1] * KVH
    partials = attend(
        queries.reshape(SEQS, ROWS, HD),
        keys.reshape(SEQS, count, HD),
        values.reshape(SEQS, count, HD),
    )
    mine = merge(exchange(partials, SPREAD), len(HOLDERS[0]), False)
    done = merge(exchange(mine, HOLDERS), len(GATHER[0]), True)
    return finish(exchange(done, GATHER))


def solution(mesh):
    placed = (P(), P(None, AXES, None, None), P(None, AXES, None, None))
    return jax.shard_map(per_device, mesh=mesh, in_specs=placed, out_specs=P(), check_vma=False)
```

```python
import functools
import math

import jax
import jax.numpy as jnp
from jax import lax
from jax.experimental import pallas as pl
from jax.experimental.pallas import tpu as pltpu
from jax.sharding import PartitionSpec as P

QH = 40
KVH = 8
HD = 128
SEQS = 2
QTOK = 4
ROWS = QTOK * QH
PIECES = 32
PIECE = SEQS * ROWS // PIECES
SLABS, SLAB = 3, 4
DONE_SLABS, DONE_SLAB = 5, 2
SCALE_LOG2 = HD ** (-0.5) * math.log2(math.e)
CHUNK = 512
LOWEST = -1e30
AXES = ("gx", "gy")
MIB = 1 << 20


def device_index(core, x, y, z):
    return ((y * 2 + z // 4) * 2 + core) * 16 + x * 4 + z % 4


def planes(order):
    return [[device_index(core, x, y, z) for core, x, y in order] for z in range(8)]


SPREAD = planes([(core, x, y) for x in (2, 1, 0, 3) for y in (2, 1, 3, 0) for core in (1, 0)])
GATHER = planes([(core, x, y) for y in (2, 1, 0, 3) for x in (2, 1, 0, 3) for core in (1, 0)])
HOLDERS = [
    [device_index(core, x, y, z) for z in (4, 3, 5, 6, 0, 1, 7, 2)]
    for core in range(2)
    for x in range(4)
    for y in range(4)
]
PIECE_OF_SLOT = [SPREAD[0].index(device) for device in GATHER[0]]


def attend_kernel(q_hbm, k_hbm, v_hbm, out_ref, q_buf, k_buf, v_buf, scores, rows, stats, q_sem, k_sem, v_sem):
    count = k_buf.shape[1]
    q_copy = pltpu.make_async_copy(q_hbm, q_buf, q_sem)
    k_copy = [pltpu.make_async_copy(k_hbm.at[s], k_buf.at[s], k_sem.at[s]) for s in range(SEQS)]
    v_copy = [pltpu.make_async_copy(v_hbm.at[s], v_buf.at[s], v_sem.at[s]) for s in range(SEQS)]
    q_copy.start()
    for s in range(SEQS):
        k_copy[s].start(priority=0)
        v_copy[s].start(priority=1)
    row = lax.broadcasted_iota(jnp.int32, (ROWS, HD), 0)
    lane = lax.broadcasted_iota(jnp.int32, (ROWS, HD), 1)
    own_head = (row % QH) // (QH // KVH) == lane % KVH
    bias = jnp.where(own_head, 0.0, LOWEST).astype(jnp.float32)
    diagonal = row % PIECE == lane
    zero = jnp.zeros((ROWS, HD), jnp.float32)

    def score(s, j, highest):
        part = lax.dot_general(
            q_buf[s],
            k_buf[s, pl.ds(j, CHUNK), :],
            (((1,), (1,)), ((), ())),
            preferred_element_type=jnp.float32,
        )
        for i in range(0, CHUNK, HD):
            own = part[:, i : i + HD] * SCALE_LOG2 + bias
            scores[s, :, pl.ds(j + i, HD)] = own
            highest = jnp.maximum(highest, own)
        return highest

    def weigh(s, j, block_max, total, block_out):
        weights = jnp.exp2(scores[s, :, pl.ds(j, CHUNK)] - block_max)
        for i in range(0, CHUNK, HD):
            total = total + weights[:, i : i + HD]
        block_out = block_out + jnp.dot(
            weights.astype(jnp.bfloat16),
            v_buf[s, pl.ds(j, CHUNK), :],
            preferred_element_type=jnp.float32,
        )
        return total, block_out

    def write(s, block_max, total, block_out):
        rows[s] = block_out
        stats[s, 0] = jnp.where(diagonal, block_max, 0.0)
        stats[s, 1] = jnp.where(diagonal, jnp.sum(total, axis=1, keepdims=True), 0.0)
        for p in range(ROWS // PIECE):
            at = s * (ROWS // PIECE) + p
            for r in range(0, PIECE, SLAB):
                n = min(SLAB, PIECE - r)
                out_ref[at, r // SLAB, 0:n, :] = rows[s, pl.ds(p * PIECE + r, n), :]
            own = pl.ds(p * PIECE, PIECE)
            for i in range(2):
                out_ref[at, SLABS - 1, SLAB - 2 + i : SLAB - 1 + i, :] = jnp.sum(stats[s, i, own, :], axis=0, keepdims=True)

    q_copy.wait()
    k_copy[0].wait()
    highest = jnp.full((ROWS, HD), LOWEST, jnp.float32)
    for j in range(0, count, CHUNK):
        highest = score(0, j, highest)
    block_max = jnp.max(highest, axis=1, keepdims=True)
    for s in range(SEQS):
        if s + 1 < SEQS:
            k_copy[s + 1].wait()
        v_copy[s].wait()
        highest = jnp.full((ROWS, HD), LOWEST, jnp.float32)
        total, block_out = zero, zero
        for j in range(0, count, CHUNK):
            if s + 1 < SEQS:
                highest = score(s + 1, j, highest)
            total, block_out = weigh(s, j, block_max, total, block_out)
        write(s, block_max, total, block_out)
        block_max = jnp.max(highest, axis=1, keepdims=True)


def attend(queries, keys, values):
    count = keys.shape[1]
    return pl.pallas_call(
        attend_kernel,
        out_shape=jax.ShapeDtypeStruct((PIECES, SLABS, SLAB, HD), jnp.float32),
        in_specs=[pl.BlockSpec(memory_space=pltpu.HBM)] * 3,
        out_specs=pl.BlockSpec(memory_space=pltpu.VMEM),
        scratch_shapes=[
            pltpu.VMEM((SEQS, ROWS, HD), jnp.bfloat16),
            pltpu.VMEM((SEQS, count, HD), jnp.bfloat16),
            pltpu.VMEM((SEQS, count, HD), jnp.bfloat16),
            pltpu.VMEM((SEQS, ROWS, count), jnp.float32),
            pltpu.VMEM((SEQS, ROWS, HD), jnp.float32),
            pltpu.VMEM((SEQS, 2, ROWS, HD), jnp.float32),
            pltpu.SemaphoreType.DMA,
            pltpu.SemaphoreType.DMA((SEQS,)),
            pltpu.SemaphoreType.DMA((SEQS,)),
        ],
        compiler_params=pltpu.CompilerParams(vmem_limit_bytes=32 * MIB),
        name="attend",
    )(*(pltpu.with_memory_space_constraint(array, pltpu.HBM) for array in (queries, keys, values)))


def merge_kernel(last, parts_ref, out_ref):
    maxima = parts_ref[:, SLABS - 1, SLAB - 2, :]
    highest = jnp.max(maxima, axis=0, keepdims=True)
    factors = jnp.exp2(maxima - highest)
    total = jnp.sum(factors * parts_ref[:, SLABS - 1, SLAB - 1, :], axis=0, keepdims=True)
    merged = []
    for r in range(PIECE):
        own = jnp.sum(parts_ref[:, r // SLAB, r % SLAB, :] * factors[:, r : r + 1], axis=0, keepdims=True)
        merged.append(own / total[:, r : r + 1] if last else own)
    slab = DONE_SLAB if last else SLAB
    merged += [] if last else [highest, total]
    for a in range(len(merged) // slab):
        rows = jnp.concatenate(merged[a * slab : (a + 1) * slab], axis=0)
        for i in range(out_ref.shape[0]):
            out_ref[i, a] = rows


def merge(parts, copies, last):
    block = (DONE_SLABS, DONE_SLAB) if last else (SLABS, SLAB)
    return pl.pallas_call(
        functools.partial(merge_kernel, last),
        out_shape=jax.ShapeDtypeStruct((copies, *block, HD), jnp.float32),
        in_specs=[pl.BlockSpec(memory_space=pltpu.VMEM)],
        out_specs=pl.BlockSpec(memory_space=pltpu.VMEM),
        compiler_params=pltpu.CompilerParams(vmem_limit_bytes=4 * MIB),
        name="merge_last" if last else "merge",
    )(parts)


def finish_kernel(pieces_ref, out_ref, rows):
    for slot, piece in enumerate(PIECE_OF_SLOT):
        for a in range(DONE_SLABS):
            rows[pl.ds(piece * PIECE + a * DONE_SLAB, DONE_SLAB), :] = pieces_ref[slot, a]
    for s in range(SEQS):
        for q in range(QTOK):
            out_ref[s, q] = rows[pl.ds((s * QTOK + q) * QH, QH), :].astype(jnp.bfloat16)


def finish(pieces):
    return pl.pallas_call(
        finish_kernel,
        out_shape=jax.ShapeDtypeStruct((SEQS, QTOK, QH, HD), jnp.bfloat16),
        in_specs=[pl.BlockSpec(memory_space=pltpu.VMEM)],
        out_specs=pl.BlockSpec(memory_space=pltpu.VMEM),
        scratch_shapes=[pltpu.VMEM((SEQS * ROWS, HD), jnp.float32)],
        compiler_params=pltpu.CompilerParams(vmem_limit_bytes=4 * MIB),
        name="finish",
    )(pieces)


def exchange(blocks, groups):
    return lax.all_to_all(blocks, AXES, 0, 0, tiled=True, axis_index_groups=groups)


def per_device(queries, keys, values):
    count = keys.shape[1] * KVH
    partials = attend(
        queries.reshape(SEQS, ROWS, HD),
        keys.reshape(SEQS, count, HD),
        values.reshape(SEQS, count, HD),
    )
    mine = merge(exchange(partials, SPREAD), len(HOLDERS[0]), False)
    done = merge(exchange(mine, HOLDERS), len(GATHER[0]), True)
    return finish(exchange(done, GATHER))


def solution(mesh):
    placed = (P(), P(None, AXES, None, None), P(None, AXES, None, None))
    return jax.shard_map(per_device, mesh=mesh, in_specs=placed, out_specs=P(), check_vma=False)
```
